128 devices in a mesh: depth: 2 (over x_hi), row: 8 (over z, core), col: 8 (over x_lo, y).
Axes of the slice: x: 4 (x_hi: 2, x_lo: 2; x = x_hi * 2 + x_lo), y: 4, z: 4, core: 2. Of those that a mesh axis runs over, the one named last changes fastest.
Arguments:
- inputs: bfloat16 [1536, 8192], P(('depth', 'col'), 'row'), may hold values from -6 to 6
- grad_out: bfloat16 [1536, 8192], P(('depth', 'col'), 'row'), may hold values from -3 to 3
- gate_weight: bfloat16 [8192, 14336], P('row', 'col'), may hold values from -0.0625 to 0.0625
- up_weight: bfloat16 [8192, 14336], P('row', 'col'), may hold values from -0.0625 to 0.0625
- down_weight: bfloat16 [14336, 8192], P('col', 'row'), may hold values from -0.046875 to 0.046875
Outputs:
- grad_in: bfloat16 [1536, 8192], P(('depth', 'col'), 'row')
- grad_gate: bfloat16 [8192, 14336], P('row', 'col')
- grad_up: bfloat16 [8192, 14336], P('row', 'col')
- grad_down: bfloat16 [14336, 8192], P('col', 'row')
The draws below stay inside these ranges and needn't reach their ends.
All inputs are finite; a program needn't handle non-finite values.
Results may differ from the reference program's by a relative error of at most 0.03.
Values may be sent and summed in bfloat16 or wider, within the bound.
A program may use at most 128 MiB of HBM per device.

```python
import jax
import jax.numpy as jnp
from jax import lax

D = 8192
FF = 14336
TOKENS = 1536
N_ROW = 8


def block_scale(stream_key, shape, pieces, least, high):
    factor_of, own = 1.0, jax.random.fold_in(stream_key, 6)
    for dim, blocks in pieces:
        steps = jnp.exp(jax.random.uniform(jax.random.fold_in(own, dim), (blocks,), jnp.float32, least / len(pieces), high / len(pieces)))
        factor_of = factor_of * jnp.repeat(steps, shape[dim] // blocks).reshape([-1 if axis == dim else 1 for axis in range(len(shape))])
    return factor_of


def scatter_about(stream_key, dims, scale, bound, shards=(), dtype=jnp.bfloat16):
    result = scale * jax.random.normal(stream_key, dims, jnp.float32)
    if shards:
        result = result * block_scale(stream_key, dims, shards, -0.22, 0.18)
    return jnp.clip(result, -bound, bound).astype(dtype)


def setup_inputs(seed: int = 0) -> dict:
    seeds = jax.random.split(jax.random.key(seed), 6)
    return {
        "inputs": scatter_about(seeds[0], (TOKENS, D), 1.0, 6.0, ((0, 16), (1, 8))),
        "grad_out": scatter_about(seeds[1], (TOKENS, D), 0.35, 3.0, ((0, 16), (1, 8))),
        "gate_weight": scatter_about(seeds[2], (D, FF), D ** -0.5, 0.0625, ((0, 8), (1, 8))),
        "up_weight": scatter_about(seeds[3], (D, FF), D ** -0.5, 0.0625, ((0, 8), (1, 8))),
        "down_weight": scatter_about(seeds[4], (FF, D), FF ** -0.5, 0.046875, ((0, 8), (1, 8))),
    }


def block_sum(operand, weight):
    block_width = operand.shape[1] // N_ROW
    running = jnp.zeros((operand.shape[0], weight.shape[1]), jnp.float32)
    for segment in range(N_ROW):
        product = jnp.dot(operand[:, segment * block_width:(segment + 1) * block_width],
                          weight[segment * block_width:(segment + 1) * block_width],
                          preferred_element_type=jnp.float32)
        rounded = lax.optimization_barrier(product.astype(jnp.bfloat16))
        running = running + rounded.astype(jnp.float32)
    return running


def reference(inputs, grad_out, gate_weight, up_weight, down_weight):
    gate_sum = block_sum(inputs, gate_weight)
    up_sum = block_sum(inputs, up_weight)
    hidden_grad = block_sum(grad_out, down_weight.T)
    sigmoid_gate = jax.nn.sigmoid(gate_sum)
    hidden = (gate_sum * sigmoid_gate * up_sum).astype(jnp.bfloat16)
    grad_gate_act = (hidden_grad * up_sum * sigmoid_gate * (1.0 + gate_sum * (1.0 - sigmoid_gate))).astype(jnp.bfloat16)
    grad_up_act = (hidden_grad * gate_sum * sigmoid_gate).astype(jnp.bfloat16)
    grad_in = (jnp.dot(grad_gate_act, gate_weight.T, preferred_element_type=jnp.float32)
               + jnp.dot(grad_up_act, up_weight.T, preferred_element_type=jnp.float32)).astype(jnp.bfloat16)
    grad_gate = jnp.dot(inputs.T, grad_gate_act, preferred_element_type=jnp.float32).astype(jnp.bfloat16)
    grad_up = jnp.dot(inputs.T, grad_up_act, preferred_element_type=jnp.float32).astype(jnp.bfloat16)
    grad_down = jnp.dot(hidden.T, grad_out, preferred_element_type=jnp.float32).astype(jnp.bfloat16)
    return grad_in, grad_gate, grad_up, grad_down
```

```python
import functools

import jax
import jax.numpy as jnp
from jax import lax
from jax.experimental import pallas as pl
from jax.experimental.pallas import tpu as pltpu
from jax.sharding import PartitionSpec as P

MESH = pl.DeviceIdType.MESH
BF16, F32 = jnp.bfloat16, jnp.float32
BLOCK = 96
CHUNK = 192
PIECE = 48
NCHUNK = 4
WIDTH = 1024
HID = 1792
HALF = 896
Y_OFFSET = (0, 1, 3, 2)
TRANS = (((1,), (1,)), ((), ()))


def multiple(value, of):
    return pl.multiple_of(value, of)


def names():
    out = ["g_xl", "g_xo", "g_x2"]
    out += [f"gy_{way}_{what}" for way in "mp2" for what in ("own", "par", "oth")]
    for j in range(NCHUNK):
        out += [f"{n}{j}" for n in (
            "core", "relA", "relB", "finA", "finB",
            "agA", "agB", "agA2", "agB2", "agX", "agXh",
            "ogA", "ogB", "ogA2", "ogB2",
            "cOwn", "cB", "cA", "cA2", "cB2",
            "oOwn", "oB", "oA", "oA2", "oB2", "oH",
            "giS", "giO",
        )]
    return {n: i for i, n in enumerate(out)}


NAMES = names()
N_FLUSH = 8 * 6 + 2


def kernel(x_in, g_in, gw_in, uw_in, dw_in,
           gin_out, x_out, g_out, a0_out, a1_out, a2_out,
           gw, uw, dw, xg, act, core_send, core_recv, part, relay, final, gi_send, gi_recv,
           send_sems, recv_sems, load_sems, flush_sems):
    d, r, c = lax.axis_index("depth"), lax.axis_index("row"), lax.axis_index("col")
    z, k = r // 2, r % 2
    xl, y = c // 4, c % 4
    za = (z + 1 + 2 * k) % 4
    zb = (z + 3 - 2 * k) % 4
    z2 = (z + 2) % 4
    core = (d, r + 1 - 2 * k, c)
    to_a, to_b = (d, za * 2 + k, c), (d, zb * 2 + k, c)
    y_m, y_p, y_2 = (y + 3) % 4, (y + 1) % 4, (y + 2) % 4
    y_dev = {"m": (d, r, xl * 4 + y_m), "p": (d, r, xl * 4 + y_p), "2": (d, r, xl * 4 + y_2)}
    diag = [(d, r, (1 - xl) * 4 + v) for v in (y_m, y_p, y_2)]
    to_xl = (d, r, (1 - xl) * 4 + y)
    to_xo = (1 - d, r, (1 - xl) * 4 + y)
    to_x2 = (1 - d, r, c)
    everyone = [core, to_a, to_b, *y_dev.values(), *diag, to_xl, to_xo, to_x2]

    started = []

    def send(name, src, dst, device):
        i = NAMES[name]
        copy = pltpu.make_async_remote_copy(
            src_ref=src, dst_ref=dst, send_sem=send_sems.at[i], recv_sem=recv_sems.at[i],
            device_id=device, device_id_type=MESH)
        copy.start()
        started.append(copy)

    def arrived(name, dst):
        i = NAMES[name]
        pltpu.make_async_remote_copy(
            src_ref=dst, dst_ref=dst, send_sem=send_sems.at[i], recv_sem=recv_sems.at[i],
            device_id=core, device_id_type=MESH).wait_recv()

    own_rows = pl.ds(multiple(xl * BLOCK, BLOCK), BLOCK)
    par_rows = pl.ds(multiple((1 - xl) * BLOCK, BLOCK), BLOCK)
    loads = [
        pltpu.make_async_copy(x_in, xg.at[0, 0, own_rows], load_sems.at[0]),
        pltpu.make_async_copy(g_in, xg.at[1, 0, own_rows], load_sems.at[1]),
        pltpu.make_async_copy(gw_in, gw, load_sems.at[2]),
        pltpu.make_async_copy(uw_in, uw, load_sems.at[3]),
        pltpu.make_async_copy(dw_in, dw, load_sems.at[4]),
    ]
    for load in loads:
        load.start()

    barrier = pltpu.get_barrier_semaphore()
    for device in everyone:
        pl.semaphore_signal(barrier, inc=1, device_id=device, device_id_type=MESH)
    pl.semaphore_wait(barrier, len(everyone))

    loads[0].wait()
    loads[1].wait()
    own = xg.at[:, 0, own_rows]
    par = xg.at[:, 0, par_rows]
    ARRIVE = {"m": 1, "p": 2, "2": 3}
    send("g_xl", own, own, to_xl)
    send("gy_m_own", own, xg.at[:, 1, own_rows], y_dev["m"])
    send("gy_p_own", own, xg.at[:, 2, own_rows], y_dev["p"])

    def gather_two():
        arrived("g_xl", par)
        send("gy_m_par", par, xg.at[:, 1, par_rows], y_dev["m"])
        send("gy_p_par", par, xg.at[:, 2, par_rows], y_dev["p"])
        send("g_xo", own, xg.at[:, 4, own_rows], to_xo)
        send("g_x2", own, xg.at[:, 4, own_rows], to_x2)

    def gather_three():
        send("gy_2_own", own, xg.at[:, 3, own_rows], y_dev["2"])
        send("gy_2_par", par, xg.at[:, 3, par_rows], y_dev["2"])

    def gather_four():
        arrived("g_x2", xg.at[:, 4, own_rows])
        arrived("g_xo", xg.at[:, 4, par_rows])
        for way in "mp2":
            send(f"gy_{way}_oth", xg.at[:, 4], xg.at[:, 4 + ARRIVE[way]], y_dev[way])

    def gathered(way):
        arrived(f"gy_{way}_own", xg.at[:, ARRIVE[way], own_rows])
        arrived(f"gy_{way}_par", xg.at[:, ARRIVE[way], par_rows])

    cols_own = pl.ds(multiple(k * HALF, 128), HALF)
    cols_par = pl.ds(multiple((1 - k) * HALF, 128), HALF)

    def products(j, cols, rows, out):
        x, g = xg[0, j], xg[1, j]
        out[0] = jnp.dot(x, gw[:, cols], preferred_element_type=F32).astype(BF16)
        out[1] = jnp.dot(x, uw[:, cols], preferred_element_type=F32).astype(BF16)
        out[2] = lax.dot_general(g, dw[rows, :], TRANS, preferred_element_type=F32).astype(BF16)

    def piece(zz):
        return pl.ds(multiple(zz * PIECE, 16), PIECE)

    p_own, p_a, p_b, p_2 = piece(z), piece(za), piece(zb), piece(z2)

    def forward(j):
        products(j, cols_par, cols_par, core_send.at[j])
        send(f"core{j}", core_send.at[j], core_recv.at[j], core)
        products(j, cols_own, cols_own, part.at[j])

    def add_core(j):
        arrived(f"core{j}", core_recv.at[j])

        def add(rows):
            part[j, :, rows] = (part[j, :, rows].astype(F32) + core_recv[j, :, rows].astype(F32)).astype(BF16)

        add(p_2)
        send(f"relA{j}", part.at[j, pl.ds(0, 2), p_2], relay.at[j, pl.ds(0, 2)], to_a)
        send(f"relB{j}", part.at[j, pl.ds(2, 1), p_2], relay.at[j, pl.ds(2, 1)], to_b)
        add(p_a)
        add(p_b)
        add(p_own)

    def add_relay(j):
        arrived(f"relA{j}", relay.at[j, pl.ds(0, 2)])
        part[j, 0:2, p_a] = (part[j, 0:2, p_a].astype(F32) + relay[j, 0:2].astype(F32)).astype(BF16)
        send(f"finA{j}", part.at[j, :, p_a], final.at[j, 0], to_a)
        arrived(f"relB{j}", relay.at[j, pl.ds(2, 1)])
        part[j, 2:3, p_b] = (part[j, 2:3, p_b].astype(F32) + relay[j, 2:3].astype(F32)).astype(BF16)
        send(f"finB{j}", part.at[j, :, p_b], final.at[j, 1], to_b)

    def activations(j):
        arrived(f"finA{j}", final.at[j, 0])
        arrived(f"finB{j}", final.at[j, 1])
        gate, up, grad = (
            part[j, t, p_own].astype(F32) + final[j, 0, t].astype(F32) + final[j, 1, t].astype(F32)
            for t in range(3))
        sig = jax.nn.sigmoid(gate)
        act[0, k, j, p_own] = (grad * up * sig * (1.0 + gate * (1.0 - sig))).astype(BF16)
        act[1, k, j, p_own] = (grad * gate * sig).astype(BF16)
        act[2, k, j, p_own] = (gate * sig * up).astype(BF16)
        mine = act.at[:, k, j, p_own]
        send(f"agA{j}", mine, mine, to_a)
        send(f"agB{j}", mine, mine, to_b)
        send(f"agX{j}", act.at[pl.ds(0, 2), k, j, p_own], act.at[pl.ds(0, 2), k, 4 + j, p_own], to_x2)
        send(f"cOwn{j}", mine, mine, core)

    def block(t, n, kk, pj, rows):
        return act.at[pl.ds(t, n), kk, pj, rows]

    def pass_on(name, ref, device):
        send(name, ref, ref, device)

    def spread_own(j):
        arrived(f"agA{j}", block(0, 3, k, j, p_b))
        pass_on(f"agA2{j}", block(0, 2, k, j, p_b), to_a)
        pass_on(f"cB{j}", block(0, 3, k, j, p_b), core)
        arrived(f"agB{j}", block(0, 3, k, j, p_a))
        pass_on(f"agB2{j}", block(2, 1, k, j, p_a), to_b)
        pass_on(f"cA{j}", block(0, 3, k, j, p_a), core)

    def spread_other(j):
        mine = block(0, 2, k, 4 + j, p_own)
        arrived(f"agX{j}", mine)
        pass_on(f"ogA{j}", mine, to_a)
        pass_on(f"ogB{j}", mine, to_b)
        pass_on(f"oOwn{j}", mine, core)

    def end_own(j):
        arrived(f"agA2{j}", block(0, 2, k, j, p_2))
        pass_on(f"cA2{j}", block(0, 2, k, j, p_2), core)
        arrived(f"agB2{j}", block(2, 1, k, j, p_2))
        pass_on(f"cB2{j}", block(2, 1, k, j, p_2), core)
        send(f"agXh{j}", act.at[2, k, j], act.at[2, k, 4 + j], to_x2)

    def relay_other(j):
        arrived(f"ogA{j}", block(0, 2, k, 4 + j, p_b))
        pass_on(f"ogA2{j}", block(0, 1, k, 4 + j, p_b), to_a)
        pass_on(f"oB{j}", block(0, 2, k, 4 + j, p_b), core)
        arrived(f"ogB{j}", block(0, 2, k, 4 + j, p_a))
        pass_on(f"ogB2{j}", block(1, 1, k, 4 + j, p_a), to_b)
        pass_on(f"oA{j}", block(0, 2, k, 4 + j, p_a), core)

    def end_other(j):
        arrived(f"ogA2{j}", block(0, 1, k, 4 + j, p_2))
        pass_on(f"oA2{j}", block(0, 1, k, 4 + j, p_2), core)
        arrived(f"ogB2{j}", block(1, 1, k, 4 + j, p_2))
        pass_on(f"oB2{j}", block(1, 1, k, 4 + j, p_2), core)
        arrived(f"agXh{j}", act.at[2, k, 4 + j])
        pass_on(f"oH{j}", act.at[2, k, 4 + j], core)

    flushes = []

    def flush(src, dst):
        copy = pltpu.make_async_copy(src, dst, flush_sems.at[len(flushes)])
        copy.start()
        flushes.append(copy)

    def flush_act(pj):
        for t, out in enumerate((a0_out, a1_out, a2_out)):
            for kk in range(2):
                flush(act.at[t, kk, pj], out.at[pj, :, pl.ds(kk * HALF, HALF)])

    def input_grad(j):
        kp = 1 - k
        arrived(f"cOwn{j}", block(0, 3, kp, j, p_own))
        arrived(f"cB{j}", block(0, 3, kp, j, p_b if False else piece((z + 3 - 2 * kp) % 4)))
        arrived(f"cA{j}", block(0, 3, kp, j, piece((z + 1 + 2 * kp) % 4)))
        arrived(f"cA2{j}", block(0, 2, kp, j, p_2))
        arrived(f"cB2{j}", block(2, 1, kp, j, p_2))
        total = None
        for t, w in enumerate((gw, uw)):
            for kk in range(2):
                term = lax.dot_general(act[t, kk, j], w[:, kk * HALF:(kk + 1) * HALF], TRANS,
                                       preferred_element_type=F32)
                total = term if total is None else total + term
        gi_send[j] = total.astype(BF16)
        yy = (y + Y_OFFSET[j]) % 4
        if j:
            send(f"giS{j}", gi_send.at[j, own_rows], gi_recv.at[2 * j], (d, r, xl * 4 + yy))
        send(f"giO{j}", gi_send.at[j, par_rows], gi_recv.at[2 * j + 1], (d, r, (1 - xl) * 4 + yy))
        flush_act(j)

    def flush_other(j):
        kp = 1 - k
        arrived(f"oOwn{j}", block(0, 2, kp, 4 + j, p_own))
        arrived(f"oB{j}", block(0, 2, kp, 4 + j, piece((z + 3 - 2 * kp) % 4)))
        arrived(f"oA{j}", block(0, 2, kp, 4 + j, piece((z + 1 + 2 * kp) % 4)))
        arrived(f"oA2{j}", block(0, 1, kp, 4 + j, p_2))
        arrived(f"oB2{j}", block(1, 1, kp, 4 + j, p_2))
        arrived(f"oH{j}", act.at[2, kp, 4 + j])
        flush_act(4 + j)

    def flush_tokens():
        for way in "mp2":
            arrived(f"gy_{way}_oth", xg.at[:, 4 + ARRIVE[way]])
        flush(xg.at[0], x_out)
        flush(xg.at[1], g_out)

    gather_two()
    for load in loads[2:]:
        load.wait()
    forward(0)
    gather_three()
    add_core(0)
    gathered("m")
    forward(1)
    add_relay(0)
    add_core(1)
    gather_four()
    activations(0)
    add_relay(1)
    spread_own(0)
    spread_other(0)
    gathered("p")
    forward(2)
    add_core(2)
    activations(1)
    end_own(0)
    add_relay(2)
    relay_other(0)
    spread_own(1)
    spread_other(1)
    gathered("2")
    forward(3)
    add_core(3)
    end_other(0)
    input_grad(0)
    activations(2)
    end_own(1)
    add_relay(3)
    relay_other(1)
    spread_own(2)
    spread_other(2)
    end_other(1)
    input_grad(1)
    flush_other(0)
    activations(3)
    end_own(2)
    relay_other(2)
    spread_own(3)
    spread_other(3)
    flush_tokens()
    end_other(2)
    input_grad(2)
    flush_other(1)
    end_own(3)
    relay_other(3)
    input_grad(3)
    flush_other(2)
    end_other(3)
    flush_other(3)

    total = gi_send[0, own_rows].astype(F32)
    for j in range(NCHUNK):
        if j:
            arrived(f"giS{j}", gi_recv.at[2 * j])
            total = total + gi_recv[2 * j].astype(F32)
        arrived(f"giO{j}", gi_recv.at[2 * j + 1])
        total = total + gi_recv[2 * j + 1].astype(F32)
    gin_out[...] = total.astype(BF16)
    for copy in started:
        copy.wait_send()
    for copy in flushes:
        copy.wait()


def per_device(inputs, grad_out, gate_weight, up_weight, down_weight):
    over_tokens = (((0,), (0,)), ((), ()))
    hbm = pl.BlockSpec(memory_space=pl.ANY)
    n = len(NAMES)
    grad_in, x, g, gate_act, up_act, hidden = pl.pallas_call(
        kernel,
        out_shape=(
            jax.ShapeDtypeStruct((BLOCK, WIDTH), BF16),
            jax.ShapeDtypeStruct((8, CHUNK, WIDTH), BF16),
            jax.ShapeDtypeStruct((8, CHUNK, WIDTH), BF16),
            jax.ShapeDtypeStruct((8, CHUNK, HID), BF16),
            jax.ShapeDtypeStruct((8, CHUNK, HID), BF16),
            jax.ShapeDtypeStruct((8, CHUNK, HID), BF16),
        ),
        in_specs=[hbm] * 5,
        out_specs=(pl.BlockSpec(memory_space=pltpu.VMEM),) + (hbm,) * 5,
        scratch_shapes=[
            pltpu.VMEM((WIDTH, HID), BF16),
            pltpu.VMEM((WIDTH, HID), BF16),
            pltpu.VMEM((HID, WIDTH), BF16),
            pltpu.VMEM((2, 8, CHUNK, WIDTH), BF16),
            pltpu.VMEM((3, 2, 8, CHUNK, HALF), BF16),
            pltpu.VMEM((NCHUNK, 3, CHUNK, HALF), BF16),
            pltpu.VMEM((NCHUNK, 3, CHUNK, HALF), BF16),
            pltpu.VMEM((NCHUNK, 3, CHUNK, HALF), BF16),
            pltpu.VMEM((NCHUNK, 3, PIECE, HALF), BF16),
            pltpu.VMEM((NCHUNK, 2, 3, PIECE, HALF), BF16),
            pltpu.VMEM((NCHUNK, CHUNK, WIDTH), BF16),
            pltpu.VMEM((8, BLOCK, WIDTH), BF16),
            pltpu.SemaphoreType.DMA((n,)),
            pltpu.SemaphoreType.DMA((n,)),
            pltpu.SemaphoreType.DMA((5,)),
            pltpu.SemaphoreType.DMA((N_FLUSH,)),
        ],
        compiler_params=pltpu.CompilerParams(
            collective_id=0, has_side_effects=True, vmem_limit_bytes=62 * 2**20),
        name="ffn_exchange",
    )(inputs, grad_out, gate_weight, up_weight, down_weight)

    def weight_grad(a, b):
        a, b = (v.reshape(v.shape[0] * v.shape[1], v.shape[2]) for v in (a, b))
        return lax.dot_general(a, b, over_tokens, preferred_element_type=F32).astype(BF16)

    return grad_in, weight_grad(x, gate_act), weight_grad(x, up_act), weight_grad(hidden, g)


def solution(mesh):
    in_specs = (
        P(("depth", "col"), "row"),
        P(("depth", "col"), "row"),
        P("row", "col"),
        P("row", "col"),
        P("col", "row"),
    )
    out_specs = (P(("depth", "col"), "row"), P("row", "col"), P("row", "col"), P("col", "row"))
    return jax.shard_map(
        per_device, mesh=mesh, in_specs=in_specs, out_specs=out_specs, check_vma=False
    )
```

```python
import jax
import jax.numpy as jnp
from jax import lax
from jax.experimental import pallas as pl
from jax.experimental.pallas import tpu as pltpu
from jax.sharding import PartitionSpec as P

MESH = pl.DeviceIdType.MESH
BF16, F32 = jnp.bfloat16, jnp.float32
BLOCK = 96
PLANE = 768
EARLY = 384
WIDTH = 1024
HID = 1792
HALF = 896
TRANS = (((1,), (1,)), ((), ()))
OVER_TOKENS = (((0,), (0,)), ((), ()))
OWN, PAR, M0, Q0, M1, Q1, T0, T1 = range(8)
CHUNKS = (192, 192, 192, 192)
BASE = tuple(sum(CHUNKS[:i]) for i in range(len(CHUNKS) + 1))
GI_GROUPS = ((OWN, PAR), (M0, Q0), (M1, Q1), (T0, T1))
ORDER = (
    ("G4",), ("G2",), ("F", 0), ("G3",), ("P", 0), ("F", 1), ("R", 0), ("P", 1), ("G5",), ("C", 0), ("R", 1),
    ("D1", 0), ("D2", 0), ("F", 2), ("P", 2), ("C", 1), ("D3", 0), ("R", 2), ("D4", 0), ("D1", 1), ("D2", 1),
    ("F", 3), ("P", 3), ("D5", 0), ("D6", 0), ("E", 0), ("C", 2), ("D3", 1), ("R", 3), ("D4", 1), ("D1", 2),
    ("D2", 2), ("D5", 1), ("D6", 1), ("E", 1), ("H", 0), ("C", 3), ("D3", 2), ("D4", 2), ("D1", 3), ("D2", 3),
    ("GF",), ("D5", 2), ("D6", 2), ("E", 2), ("H", 1), ("W", 0, 0), ("W", 0, 1), ("D3", 3), ("W", 0, 2),
    ("W", 0, 3), ("W", 1, 0), ("D4", 3), ("W", 1, 1), ("W", 1, 2), ("W", 1, 3), ("V", 0, 0), ("E", 3),
    ("V", 0, 1), ("V", 0, 2), ("V", 0, 3), ("H", 2), ("D5", 3), ("V", 1, 0), ("V", 1, 1), ("D6", 3),
    ("V", 1, 2), ("V", 1, 3), ("H", 3),
)
STEPS = (
    "core", "relA", "relB", "finA", "finB", "agA", "agB", "agA2", "agB2", "agX", "agXh",
    "ogA", "ogB", "ogA2", "ogB2", "cOwn", "cB", "cA", "cA2", "cB2", "oOwn", "oB", "oA", "oA2", "oB2", "oH",
)


def names():
    out = ["g_xl", "g_xo", "g_x2"]
    out += [f"gy_{way}_{what}" for way in "mp2" for what in ("own", "par", "oth0", "oth1")]
    out += [f"gi{b}" for b in range(1, 8)]
    for j in range(len(CHUNKS)):
        out += [f"{n}{j}" for n in STEPS]
    return {n: i for i, n in enumerate(out)}


NAMES = names()
N_FLUSH = 2 * len(CHUNKS) * 6 + 2


def multiple(value, of):
    return pl.multiple_of(value, of)


def rows_of(block, count=1):
    return pl.ds(block * BLOCK, count * BLOCK)


def place(plane, row):
    return plane * EARLY + row + (EARLY if row >= EARLY else 0)


def kernel(x_in, g_in, gw_in, uw_in, dw_in,
           gin_out, x_out, g_out, a0_out, a1_out, a2_out, p0_out, p1_out, p2_out,
           gw, uw, dw, xg, act, core_send, core_recv, part, relay, final, gi_send, gi_recv, wg,
           send_sems, recv_sems, load_sems, flush_sems, wg_sems):
    d, r, c = lax.axis_index("depth"), lax.axis_index("row"), lax.axis_index("col")
    z, k = r // 2, r % 2
    kp = 1 - k
    xl, y = c // 4, c % 4
    za = (z + 1 + 2 * k) % 4
    zb = (z + 3 - 2 * k) % 4
    z2 = (z + 2) % 4
    core = (d, r + 1 - 2 * k, c)
    to_a, to_b = (d, za * 2 + k, c), (d, zb * 2 + k, c)
    y_m, y_p, y_2 = (y + 3) % 4, (y + 1) % 4, (y + 2) % 4
    same = {w: (d, r, xl * 4 + v) for w, v in (("m", y_m), ("p", y_p), ("2", y_2))}
    diag = {w: (d, r, (1 - xl) * 4 + v) for w, v in (("m", y_m), ("p", y_p), ("2", y_2))}
    to_xl = (d, r, (1 - xl) * 4 + y)
    to_xo = (1 - d, r, (1 - xl) * 4 + y)
    to_x2 = (1 - d, r, c)
    everyone = [core, to_a, to_b, *same.values(), *diag.values(), to_xl, to_xo, to_x2]
    at_own = {"m": Q0, "p": M0, "2": T0}
    at_par = {"m": Q1, "p": M1, "2": T1}

    started = []

    def send(name, src, dst, device):
        i = NAMES[name]
        copy = pltpu.make_async_remote_copy(
            src_ref=src, dst_ref=dst, send_sem=send_sems.at[i], recv_sem=recv_sems.at[i],
            device_id=device, device_id_type=MESH)
        copy.start()
        started.append(copy)

    def arrived(name, dst):
        i = NAMES[name]
        pltpu.make_async_remote_copy(
            src_ref=dst, dst_ref=dst, send_sem=send_sems.at[i], recv_sem=recv_sems.at[i],
            device_id=core, device_id_type=MESH).wait_recv()

    loads = [
        pltpu.make_async_copy(x_in, xg.at[0, rows_of(OWN)], load_sems.at[0]),
        pltpu.make_async_copy(g_in, xg.at[1, rows_of(OWN)], load_sems.at[1]),
        pltpu.make_async_copy(gw_in, gw, load_sems.at[2]),
        pltpu.make_async_copy(uw_in, uw, load_sems.at[3]),
        pltpu.make_async_copy(dw_in, dw, load_sems.at[4]),
    ]
    for load in loads:
        load.start()

    barrier = pltpu.get_barrier_semaphore()
    for device in everyone:
        pl.semaphore_signal(barrier, inc=1, device_id=device, device_id_type=MESH)
    pl.semaphore_wait(barrier, len(everyone))

    def tokens(block, plane=0):
        return xg.at[:, pl.ds(place(plane, block * BLOCK), BLOCK)]

    loads[0].wait()
    loads[1].wait()
    send("g_xl", tokens(OWN), tokens(PAR), to_xl)
    for way in "mp":
        send(f"gy_{way}_own", tokens(OWN), tokens(at_own[way]), same[way])

    def gather_par():
        arrived("g_xl", tokens(PAR))
        for way in "mp":
            send(f"gy_{way}_par", tokens(PAR), tokens(at_par[way]), same[way])

    def gather_far():
        send("gy_2_own", tokens(OWN), tokens(at_own["2"]), same["2"])
        send("gy_2_par", tokens(PAR), tokens(at_par["2"]), same["2"])

    def gather_depth():
        send("g_x2", tokens(OWN), tokens(OWN, 1), to_x2)
        send("g_xo", tokens(OWN), tokens(PAR, 1), to_xo)

    def gather_other():
        arrived("g_x2", tokens(OWN, 1))
        arrived("g_xo", tokens(PAR, 1))
        for way in "mp2":
            send(f"gy_{way}_oth0", tokens(OWN, 1), tokens(at_own[way], 1), same[way])
            send(f"gy_{way}_oth1", tokens(PAR, 1), tokens(at_par[way], 1), same[way])

    seen = set()
    source = {M0: "gy_p_own", Q0: "gy_m_own", M1: "gy_p_par", Q1: "gy_m_par", T0: "gy_2_own", T1: "gy_2_par"}

    def gathered(block):
        if block in source and block not in seen:
            seen.add(block)
            arrived(source[block], tokens(block))

    cols_own = pl.ds(multiple(k * HALF, 128), HALF)
    cols_par = pl.ds(multiple(kp * HALF, 128), HALF)

    def chunk(j):
        return pl.ds(BASE[j], CHUNKS[j])

    def products(j, cols, out):
        here = pl.ds(place(0, BASE[j]), CHUNKS[j])
        x, g = xg[0, here], xg[1, here]
        out[0, chunk(j)] = jnp.dot(x, gw[:, cols], preferred_element_type=F32).astype(BF16)
        out[1, chunk(j)] = jnp.dot(x, uw[:, cols], preferred_element_type=F32).astype(BF16)
        out[2, chunk(j)] = lax.dot_general(g, dw[cols, :], TRANS, preferred_element_type=F32).astype(BF16)

    def piece(j, zz):
        size = CHUNKS[j] // 4
        return pl.ds(multiple(BASE[j] + zz * size, 16), size)

    def act_piece(j, zz, plane=0):
        size = CHUNKS[j] // 4
        return pl.ds(multiple(place(plane, BASE[j]) + zz * size, 16), size)

    def slot(j):
        return pl.ds(BASE[j] // 4, CHUNKS[j] // 4)

    def whole(j):
        return core_recv.at[:, chunk(j)]

    def forward(j):
        for b in range(8):
            if b * BLOCK < BASE[j + 1] and (b + 1) * BLOCK > BASE[j]:
                gathered(b)
        if j == 0:
            for load in loads[2:]:
                load.wait()
        products(j, cols_par, core_send)
        send(f"core{j}", core_send.at[:, chunk(j)], whole(j), core)
        products(j, cols_own, part)

    def add_core(j):
        arrived(f"core{j}", whole(j))

        def add(zz):
            rows = piece(j, zz)
            part[:, rows] = (part[:, rows].astype(F32) + core_recv[:, rows].astype(F32)).astype(BF16)

        add(z2)
        send(f"relA{j}", part.at[pl.ds(0, 2), piece(j, z2)], relay.at[pl.ds(0, 2), slot(j)], to_a)
        send(f"relB{j}", part.at[pl.ds(2, 1), piece(j, z2)], relay.at[pl.ds(2, 1), slot(j)], to_b)
        add(za)
        add(zb)
        add(z)

    def add_relay(j):
        rows_a, rows_b = piece(j, za), piece(j, zb)
        arrived(f"relA{j}", relay.at[pl.ds(0, 2), slot(j)])
        part[0:2, rows_a] = (part[0:2, rows_a].astype(F32) + relay[0:2, slot(j)].astype(F32)).astype(BF16)
        send(f"finA{j}", part.at[:, rows_a], final.at[0, :, slot(j)], to_a)
        arrived(f"relB{j}", relay.at[pl.ds(2, 1), slot(j)])
        part[2:3, rows_b] = (part[2:3, rows_b].astype(F32) + relay[2:3, slot(j)].astype(F32)).astype(BF16)
        send(f"finB{j}", part.at[:, rows_b], final.at[1, :, slot(j)], to_b)

    def block(t, n, kk, j, zz, plane=0):
        return act.at[pl.ds(t, n), kk, act_piece(j, zz, plane)]

    def pass_on(name, ref, device):
        send(name, ref, ref, device)

    def activations(j):
        arrived(f"finA{j}", final.at[0, :, slot(j)])
        arrived(f"finB{j}", final.at[1, :, slot(j)])
        mine = piece(j, z)
        gate, up, grad = (
            part[t, mine].astype(F32) + final[0, t, slot(j)].astype(F32) + final[1, t, slot(j)].astype(F32)
            for t in range(3))
        sig = jax.nn.sigmoid(gate)
        here = act_piece(j, z)
        act[0, k, here] = (grad * up * sig * (1.0 + gate * (1.0 - sig))).astype(BF16)
        act[1, k, here] = (grad * gate * sig).astype(BF16)
        act[2, k, here] = (gate * sig * up).astype(BF16)
        pass_on(f"agA{j}", block(0, 3, k, j, z), to_a)
        pass_on(f"agB{j}", block(0, 3, k, j, z), to_b)
        send(f"agX{j}", block(0, 2, k, j, z), block(0, 2, k, j, z, 1), to_x2)
        pass_on(f"cOwn{j}", block(0, 3, k, j, z), core)

    def spread_own(j):
        arrived(f"agA{j}", block(0, 3, k, j, zb))
        pass_on(f"agA2{j}", block(0, 2, k, j, zb), to_a)
        pass_on(f"cB{j}", block(0, 3, k, j, zb), core)
        arrived(f"agB{j}", block(0, 3, k, j, za))
        pass_on(f"agB2{j}", block(2, 1, k, j, za), to_b)
        pass_on(f"cA{j}", block(0, 3, k, j, za), core)

    def spread_other(j):
        mine = block(0, 2, k, j, z, 1)
        arrived(f"agX{j}", mine)
        pass_on(f"ogA{j}", mine, to_a)
        pass_on(f"ogB{j}", mine, to_b)
        pass_on(f"oOwn{j}", mine, core)

    def hidden_rows(j, kk, plane):
        return act.at[2, kk, pl.ds(place(plane, BASE[j]), CHUNKS[j])]

    def end_own(j):
        arrived(f"agA2{j}", block(0, 2, k, j, z2))
        pass_on(f"cA2{j}", block(0, 2, k, j, z2), core)
        arrived(f"agB2{j}", block(2, 1, k, j, z2))
        pass_on(f"cB2{j}", block(2, 1, k, j, z2), core)
        send(f"agXh{j}", hidden_rows(j, k, 0), hidden_rows(j, k, 1), to_x2)

    def relay_other(j):
        arrived(f"ogA{j}", block(0, 2, k, j, zb, 1))
        pass_on(f"ogA2{j}", block(0, 1, k, j, zb, 1), to_a)
        pass_on(f"oB{j}", block(0, 2, k, j, zb, 1), core)
        arrived(f"ogB{j}", block(0, 2, k, j, za, 1))
        pass_on(f"ogB2{j}", block(1, 1, k, j, za, 1), to_b)
        pass_on(f"oA{j}", block(0, 2, k, j, za, 1), core)

    def end_other(j):
        arrived(f"ogA2{j}", block(0, 1, k, j, z2, 1))
        pass_on(f"oA2{j}", block(0, 1, k, j, z2, 1), core)
        arrived(f"ogB2{j}", block(1, 1, k, j, z2, 1))
        pass_on(f"oB2{j}", block(1, 1, k, j, z2, 1), core)

    def end_hidden(j):
        arrived(f"agXh{j}", hidden_rows(j, k, 1))
        pass_on(f"oH{j}", hidden_rows(j, k, 1), core)

    flushes = []

    def flush(src, dst):
        copy = pltpu.make_async_copy(src, dst, flush_sems.at[len(flushes)])
        copy.start()
        flushes.append(copy)

    def flush_act(j, plane):
        if BASE[j] < EARLY:
            return
        rows = pl.ds(place(plane, BASE[j]), CHUNKS[j])
        to_rows = pl.ds(place(plane, BASE[j]) - 2 * EARLY, CHUNKS[j])
        for t, out in enumerate((a0_out, a1_out, a2_out)):
            for kk in range(2):
                flush(act.at[t, kk, rows], out.at[to_rows, pl.ds(kk * HALF, HALF)])

    complete = set()

    def own_complete(j):
        if j in complete:
            return
        complete.add(j)
        arrived(f"cOwn{j}", block(0, 3, kp, j, z))
        arrived(f"cB{j}", block(0, 3, kp, j, za))
        arrived(f"cA{j}", block(0, 3, kp, j, zb))
        arrived(f"cA2{j}", block(0, 2, kp, j, z2))
        arrived(f"cB2{j}", block(2, 1, kp, j, z2))
        flush_act(j, 0)

    def other_complete(j):
        arrived(f"oOwn{j}", block(0, 2, kp, j, z, 1))
        arrived(f"oB{j}", block(0, 2, kp, j, za, 1))
        arrived(f"oA{j}", block(0, 2, kp, j, zb, 1))
        arrived(f"oA2{j}", block(0, 1, kp, j, z2, 1))
        arrived(f"oB2{j}", block(1, 1, kp, j, z2, 1))
        arrived(f"oH{j}", hidden_rows(j, kp, 1))
        flush_act(j, 1)

    gi_to = {PAR: to_xl, M0: same["m"], Q0: same["p"], M1: diag["m"], Q1: diag["p"], T0: same["2"], T1: diag["2"]}

    def input_grad(i):
        group = GI_GROUPS[i]
        first, end = group[0] * BLOCK, (group[-1] + 1) * BLOCK
        for j in range(len(CHUNKS)):
            if BASE[j] < end and BASE[j + 1] > first:
                own_complete(j)
        rows = pl.ds(first, end - first)
        act_rows = pl.ds(place(0, first), end - first)
        total = None
        for t, w in enumerate((gw, uw)):
            for kk in range(2):
                term = lax.dot_general(act[t, kk, act_rows], w[:, kk * HALF:(kk + 1) * HALF], TRANS,
                                       preferred_element_type=F32)
                total = term if total is None else total + term
        gi_send[rows] = total.astype(BF16)
        for b in group:
            if b != OWN:
                send(f"gi{b}", gi_send.at[rows_of(b)], gi_recv.at[b], gi_to[b])

    def flush_tokens():
        for way in "mp2":
            arrived(f"gy_{way}_oth0", tokens(at_own[way], 1))
            arrived(f"gy_{way}_oth1", tokens(at_par[way], 1))
        late = pl.ds(2 * EARLY, 2 * (PLANE - EARLY))
        flush(xg.at[0, late], x_out)
        flush(xg.at[1, late], g_out)

    wg_copies = []

    def wg_slot():
        n = len(wg_copies)
        if n >= 4:
            wg_copies[n - 4].wait()
        return n % 4

    def wg_store(src, dst):
        copy = pltpu.make_async_copy(src, dst, wg_sems.at[len(wg_copies)])
        copy.start()
        wg_copies.append(copy)

    early = pl.ds(0, 2 * EARLY)

    def weight_grad_in(t, m):
        i = wg_slot()
        lhs = xg[0, early, m * 256:(m + 1) * 256]
        for kk in range(2):
            wg[i, :, kk * HALF:(kk + 1) * HALF] = lax.dot_general(
                lhs, act[t, kk, early], OVER_TOKENS, preferred_element_type=F32).astype(BF16)
        wg_store(wg.at[i], (p0_out, p1_out)[t].at[pl.ds(m * 256, 256)])

    def weight_grad_down(kk, m):
        i = wg_slot()
        size = min(256, HALF - m * 256)
        wg[i, :size, :WIDTH] = lax.dot_general(
            act[2, kk, early, m * 256:m * 256 + size], xg[1, early], OVER_TOKENS,
            preferred_element_type=F32).astype(BF16)
        wg_store(wg.at[i, pl.ds(0, size), pl.ds(0, WIDTH)], p2_out.at[pl.ds(kk * HALF + m * 256, size)])

    stages = {
        "G2": gather_par, "G3": gather_far, "G4": gather_depth, "G5": gather_other, "GF": flush_tokens,
        "F": forward, "P": add_core, "R": add_relay, "C": activations, "D1": spread_own, "D2": spread_other,
        "D3": end_own, "D4": relay_other, "D5": end_other, "D6": end_hidden, "H": other_complete,
        "E": input_grad, "W": weight_grad_in, "V": weight_grad_down,
    }
    for name, *index in ORDER:
        stages[name](*index)

    total = gi_send[rows_of(OWN)].astype(F32)
    for b in range(1, 8):
        arrived(f"gi{b}", gi_recv.at[b])
        total = total + gi_recv[b].astype(F32)
    gin_out[...] = total.astype(BF16)
    for copy in started:
        copy.wait_send()
    for copy in flushes + wg_copies[-4:]:
        copy.wait()


def per_device(inputs, grad_out, gate_weight, up_weight, down_weight):
    hbm = pl.BlockSpec(memory_space=pl.ANY)
    n = len(NAMES)
    tokens = 2 * PLANE
    late = tokens - 2 * EARLY
    grad_in, x, g, gate_act, up_act, hidden, gate_early, up_early, down_early = pl.pallas_call(
        kernel,
        out_shape=(
            jax.ShapeDtypeStruct((BLOCK, WIDTH), BF16),
            jax.ShapeDtypeStruct((late, WIDTH), BF16),
            jax.ShapeDtypeStruct((late, WIDTH), BF16),
            jax.ShapeDtypeStruct((late, HID), BF16),
            jax.ShapeDtypeStruct((late, HID), BF16),
            jax.ShapeDtypeStruct((late, HID), BF16),
            jax.ShapeDtypeStruct((WIDTH, HID), BF16),
            jax.ShapeDtypeStruct((WIDTH, HID), BF16),
            jax.ShapeDtypeStruct((HID, WIDTH), BF16),
        ),
        in_specs=[hbm] * 5,
        out_specs=(pl.BlockSpec(memory_space=pltpu.VMEM),) + (hbm,) * 8,
        scratch_shapes=[
            pltpu.VMEM((WIDTH, HID), BF16),
            pltpu.VMEM((WIDTH, HID), BF16),
            pltpu.VMEM((HID, WIDTH), BF16),
            pltpu.VMEM((2, tokens, WIDTH), BF16),
            pltpu.VMEM((3, 2, tokens, HALF), BF16),
            pltpu.VMEM((3, PLANE, HALF), BF16),
            pltpu.VMEM((3, PLANE, HALF), BF16),
            pltpu.VMEM((3, PLANE, HALF), BF16),
            pltpu.VMEM((3, PLANE // 4, HALF), BF16),
            pltpu.VMEM((2, 3, PLANE // 4, HALF), BF16),
            pltpu.VMEM((PLANE, WIDTH), BF16),
            pltpu.VMEM((8, BLOCK, WIDTH), BF16),
            pltpu.VMEM((4, 256, HID), BF16),
            pltpu.SemaphoreType.DMA((n,)),
            pltpu.SemaphoreType.DMA((n,)),
            pltpu.SemaphoreType.DMA((5,)),
            pltpu.SemaphoreType.DMA((N_FLUSH,)),
            pltpu.SemaphoreType.DMA((16,)),
        ],
        compiler_params=pltpu.CompilerParams(
            collective_id=0, has_side_effects=True, vmem_limit_bytes=62 * 2**20),
        name="ffn_exchange",
    )(inputs, grad_out, gate_weight, up_weight, down_weight)

    def weight_grad(a, b, rest):
        late_sum = lax.dot_general(a, b, OVER_TOKENS, preferred_element_type=F32)
        return (late_sum + rest.astype(F32)).astype(BF16)

    return (
        grad_in,
        weight_grad(x, gate_act, gate_early),
        weight_grad(x, up_act, up_early),
        weight_grad(hidden, g, down_early),
    )


def solution(mesh):
    in_specs = (
        P(("depth", "col"), "row"),
        P(("depth", "col"), "row"),
        P("row", "col"),
        P("row", "col"),
        P("col", "row"),
    )
    out_specs = (P(("depth", "col"), "row"), P("row", "col"), P("row", "col"), P("col", "row"))
    return jax.shard_map(
        per_device, mesh=mesh, in_specs=in_specs, out_specs=out_specs, check_vma=False
    )
```

```python
import jax
import jax.numpy as jnp
from jax import lax
from jax.experimental import pallas as pl
from jax.experimental.pallas import tpu as pltpu
from jax.sharding import PartitionSpec as P

MESH = pl.DeviceIdType.MESH
BF16, F32 = jnp.bfloat16, jnp.float32
BLOCK = 96
PLANE = 768
EARLY = 384
WIDTH = 1024
HID = 1792
HALF = 896
TRANS = (((1,), (1,)), ((), ()))
OVER_TOKENS = (((0,), (0,)), ((), ()))
OWN, PAR, M0, Q0, M1, Q1, T0, T1 = range(8)
CHUNKS = (64, 128, 192, 192, 192)
BASE = tuple(sum(CHUNKS[:i]) for i in range(len(CHUNKS) + 1))
PIECEWISE = (len(CHUNKS) - 1,)
CROSS = tuple(3 if j in PIECEWISE else 2 for j in range(len(CHUNKS)))
GI_GROUPS = ((OWN, PAR), (M0, Q0), (M1, Q1), (T0, T1))
ORDER = (
    ("G4",), ("F", 0), ("P", 0), ("R", 0), ("G2",), ("F", 1), ("C", 0), ("G3",), ("P", 1), ("D1", 0),
    ("D2", 0), ("F", 2), ("R", 1), ("P", 2), ("C", 1), ("G5",), ("D3", 0), ("D4", 0), ("R", 2), ("D5", 0),
    ("D6", 0), ("D1", 1), ("D2", 1), ("F", 3), ("P", 3), ("C", 2), ("R", 3), ("D3", 1), ("D4", 1), ("D1", 2),
    ("D2", 2), ("F", 4), ("P", 4), ("D5", 1), ("D6", 1), ("H", 0), ("E", 0), ("C", 3), ("R", 4), ("D3", 2),
    ("D4", 2), ("D1", 3), ("D2", 3), ("D5", 2), ("D6", 2), ("E", 1), ("H", 1), ("C", 4), ("D3", 3), ("D4", 3),
    ("D1", 4), ("D2", 4), ("GF",), ("D5", 3), ("D6", 3), ("E", 2), ("H", 2), ("W", 0, 0), ("W", 0, 1),
    ("D3", 4), ("W", 0, 2), ("W", 0, 3), ("D4", 4), ("W", 1, 0), ("W", 1, 1), ("E", 3), ("W", 1, 2),
    ("W", 1, 3), ("D5", 4), ("D6", 4), ("V", 0, 0), ("V", 0, 1), ("V", 0, 2), ("H", 3), ("V", 0, 3),
    ("V", 1, 0), ("V", 1, 1), ("V", 1, 2), ("V", 1, 3), ("H", 4),
)
STEPS = (
    "core", "relA", "relB", "finA", "finB", "agA", "agB", "agA2", "agB2", "agX", "agXh",
    "ogA", "ogB", "ogA2", "ogB2", "cOwn", "cB", "cA", "cA2", "cB2", "oOwn", "oB", "oA", "oA2", "oB2", "oH",
)


def names():
    out = ["g_xl", "g_xo", "g_x2"]
    out += [f"gy_{way}_{what}" for way in "mp2" for what in ("own", "par", "oth0", "oth1")]
    out += [f"gi{b}" for b in range(1, 8)]
    for j in range(len(CHUNKS)):
        out += [f"{n}{j}" for n in STEPS if CROSS[j] == 2 or n not in ("agXh", "oH")]
    return {n: i for i, n in enumerate(out)}


NAMES = names()
N_FLUSH = 2 * len(CHUNKS) * 6 + 2


def multiple(value, of):
    return pl.multiple_of(value, of)


def rows_of(block, count=1):
    return pl.ds(block * BLOCK, count * BLOCK)


def place(plane, row):
    return plane * EARLY + row + (EARLY if row >= EARLY else 0)


def kernel(x_in, g_in, gw_in, uw_in, dw_in,
           gin_out, x_out, g_out, a0_out, a1_out, a2_out, p0_out, p1_out, p2_out,
           gw, uw, dw, xg, act, core_send, core_recv, part, relay, final, gi_send, gi_recv, wg,
           send_sems, recv_sems, load_sems, flush_sems, wg_sems):
    d, r, c = lax.axis_index("depth"), lax.axis_index("row"), lax.axis_index("col")
    z, k = r // 2, r % 2
    kp = 1 - k
    xl, y = c // 4, c % 4
    za = (z + 1 + 2 * k) % 4
    zb = (z + 3 - 2 * k) % 4
    z2 = (z + 2) % 4
    core = (d, r + 1 - 2 * k, c)
    to_a, to_b = (d, za * 2 + k, c), (d, zb * 2 + k, c)
    y_m, y_p, y_2 = (y + 3) % 4, (y + 1) % 4, (y + 2) % 4
    same = {w: (d, r, xl * 4 + v) for w, v in (("m", y_m), ("p", y_p), ("2", y_2))}
    diag = {w: (d, r, (1 - xl) * 4 + v) for w, v in (("m", y_m), ("p", y_p), ("2", y_2))}
    to_xl = (d, r, (1 - xl) * 4 + y)
    to_xo = (1 - d, r, (1 - xl) * 4 + y)
    to_x2 = (1 - d, r, c)
    everyone = [core, to_a, to_b, *same.values(), *diag.values(), to_xl, to_xo, to_x2]
    at_own = {"m": Q0, "p": M0, "2": T0}
    at_par = {"m": Q1, "p": M1, "2": T1}

    started = []

    def send(name, src, dst, device):
        i = NAMES[name]
        copy = pltpu.make_async_remote_copy(
            src_ref=src, dst_ref=dst, send_sem=send_sems.at[i], recv_sem=recv_sems.at[i],
            device_id=device, device_id_type=MESH)
        copy.start()
        started.append(copy)

    def arrived(name, dst):
        i = NAMES[name]
        pltpu.make_async_remote_copy(
            src_ref=dst, dst_ref=dst, send_sem=send_sems.at[i], recv_sem=recv_sems.at[i],
            device_id=core, device_id_type=MESH).wait_recv()

    loads = [
        pltpu.make_async_copy(x_in, xg.at[0, rows_of(OWN)], load_sems.at[0]),
        pltpu.make_async_copy(g_in, xg.at[1, rows_of(OWN)], load_sems.at[1]),
        pltpu.make_async_copy(gw_in, gw, load_sems.at[2]),
        pltpu.make_async_copy(uw_in, uw, load_sems.at[3]),
        pltpu.make_async_copy(dw_in, dw, load_sems.at[4]),
    ]
    for load in loads:
        load.start()

    barrier = pltpu.get_barrier_semaphore()
    for device in everyone:
        pl.semaphore_signal(barrier, inc=1, device_id=device, device_id_type=MESH)
    pl.semaphore_wait(barrier, len(everyone))

    def tokens(block, plane=0):
        return xg.at[:, pl.ds(place(plane, block * BLOCK), BLOCK)]

    loads[0].wait()
    loads[1].wait()
    send("g_xl", tokens(OWN), tokens(PAR), to_xl)
    for way in "mp":
        send(f"gy_{way}_own", tokens(OWN), tokens(at_own[way]), same[way])

    def gather_par():
        arrived("g_xl", tokens(PAR))
        for way in "mp":
            send(f"gy_{way}_par", tokens(PAR), tokens(at_par[way]), same[way])

    def gather_far():
        send("gy_2_own", tokens(OWN), tokens(at_own["2"]), same["2"])
        send("gy_2_par", tokens(PAR), tokens(at_par["2"]), same["2"])

    def gather_depth():
        send("g_x2", tokens(OWN), tokens(OWN, 1), to_x2)
        send("g_xo", tokens(OWN), tokens(PAR, 1), to_xo)

    def gather_other():
        arrived("g_x2", tokens(OWN, 1))
        arrived("g_xo", tokens(PAR, 1))
        for way in "mp2":
            send(f"gy_{way}_oth0", tokens(OWN, 1), tokens(at_own[way], 1), same[way])
            send(f"gy_{way}_oth1", tokens(PAR, 1), tokens(at_par[way], 1), same[way])

    seen = set()
    source = {M0: "gy_p_own", Q0: "gy_m_own", M1: "gy_p_par", Q1: "gy_m_par", T0: "gy_2_own", T1: "gy_2_par"}

    def gathered(block):
        if block in source and block not in seen:
            seen.add(block)
            arrived(source[block], tokens(block))

    cols_own = pl.ds(multiple(k * HALF, 128), HALF)
    cols_par = pl.ds(multiple(kp * HALF, 128), HALF)

    def chunk(j):
        return pl.ds(BASE[j], CHUNKS[j])

    def products(j, cols, out):
        here = pl.ds(place(0, BASE[j]), CHUNKS[j])
        x, g = xg[0, here], xg[1, here]
        out[0, chunk(j)] = jnp.dot(x, gw[:, cols], preferred_element_type=F32).astype(BF16)
        out[1, chunk(j)] = jnp.dot(x, uw[:, cols], preferred_element_type=F32).astype(BF16)
        out[2, chunk(j)] = lax.dot_general(g, dw[cols, :], TRANS, preferred_element_type=F32).astype(BF16)

    def piece(j, zz):
        size = CHUNKS[j] // 4
        return pl.ds(multiple(BASE[j] + zz * size, 16), size)

    def act_piece(j, zz, plane=0):
        size = CHUNKS[j] // 4
        return pl.ds(multiple(place(plane, BASE[j]) + zz * size, 16), size)

    def slot(j):
        return pl.ds(BASE[j] // 4, CHUNKS[j] // 4)

    def whole(j):
        return core_recv.at[:, chunk(j)]

    def forward(j):
        for b in range(8):
            if b * BLOCK < BASE[j + 1] and (b + 1) * BLOCK > BASE[j]:
                gathered(b)
        if j == 0:
            for load in loads[2:]:
                load.wait()
        products(j, cols_par, core_send)
        send(f"core{j}", core_send.at[:, chunk(j)], whole(j), core)
        products(j, cols_own, part)

    def add_core(j):
        arrived(f"core{j}", whole(j))

        def add(zz):
            rows = piece(j, zz)
            part[:, rows] = (part[:, rows].astype(F32) + core_recv[:, rows].astype(F32)).astype(BF16)

        add(z2)
        send(f"relA{j}", part.at[pl.ds(0, 2), piece(j, z2)], relay.at[pl.ds(0, 2), slot(j)], to_a)
        send(f"relB{j}", part.at[pl.ds(2, 1), piece(j, z2)], relay.at[pl.ds(2, 1), slot(j)], to_b)
        add(za)
        add(zb)
        add(z)

    def add_relay(j):
        rows_a, rows_b = piece(j, za), piece(j, zb)
        arrived(f"relA{j}", relay.at[pl.ds(0, 2), slot(j)])
        part[0:2, rows_a] = (part[0:2, rows_a].astype(F32) + relay[0:2, slot(j)].astype(F32)).astype(BF16)
        send(f"finA{j}", part.at[:, rows_a], final.at[0, :, slot(j)], to_a)
        arrived(f"relB{j}", relay.at[pl.ds(2, 1), slot(j)])
        part[2:3, rows_b] = (part[2:3, rows_b].astype(F32) + relay[2:3, slot(j)].astype(F32)).astype(BF16)
        send(f"finB{j}", part.at[:, rows_b], final.at[1, :, slot(j)], to_b)

    def block(t, n, kk, j, zz, plane=0):
        return act.at[pl.ds(t, n), kk, act_piece(j, zz, plane)]

    def pass_on(name, ref, device):
        send(name, ref, ref, device)

    def activations(j):
        arrived(f"finA{j}", final.at[0, :, slot(j)])
        arrived(f"finB{j}", final.at[1, :, slot(j)])
        mine = piece(j, z)
        gate, up, grad = (
            part[t, mine].astype(F32) + final[0, t, slot(j)].astype(F32) + final[1, t, slot(j)].astype(F32)
            for t in range(3))
        sig = jax.nn.sigmoid(gate)
        here = act_piece(j, z)
        act[0, k, here] = (grad * up * sig * (1.0 + gate * (1.0 - sig))).astype(BF16)
        act[1, k, here] = (grad * gate * sig).astype(BF16)
        act[2, k, here] = (gate * sig * up).astype(BF16)
        pass_on(f"agA{j}", block(0, 3, k, j, z), to_a)
        pass_on(f"agB{j}", block(0, 3, k, j, z), to_b)
        send(f"agX{j}", block(0, CROSS[j], k, j, z), block(0, CROSS[j], k, j, z, 1), to_x2)
        pass_on(f"cOwn{j}", block(0, 3, k, j, z), core)

    def spread_own(j):
        arrived(f"agA{j}", block(0, 3, k, j, zb))
        pass_on(f"agA2{j}", block(0, 2, k, j, zb), to_a)
        pass_on(f"cB{j}", block(0, 3, k, j, zb), core)
        arrived(f"agB{j}", block(0, 3, k, j, za))
        pass_on(f"agB2{j}", block(2, 1, k, j, za), to_b)
        pass_on(f"cA{j}", block(0, 3, k, j, za), core)

    def spread_other(j):
        mine = block(0, CROSS[j], k, j, z, 1)
        arrived(f"agX{j}", mine)
        pass_on(f"ogA{j}", mine, to_a)
        pass_on(f"ogB{j}", mine, to_b)
        pass_on(f"oOwn{j}", mine, core)

    def hidden_rows(j, kk, plane):
        return act.at[2, kk, pl.ds(place(plane, BASE[j]), CHUNKS[j])]

    def end_own(j):
        arrived(f"agA2{j}", block(0, 2, k, j, z2))
        pass_on(f"cA2{j}", block(0, 2, k, j, z2), core)
        arrived(f"agB2{j}", block(2, 1, k, j, z2))
        pass_on(f"cB2{j}", block(2, 1, k, j, z2), core)
        if CROSS[j] == 2:
            send(f"agXh{j}", hidden_rows(j, k, 0), hidden_rows(j, k, 1), to_x2)

    def relay_other(j):
        n = CROSS[j]
        arrived(f"ogA{j}", block(0, n, k, j, zb, 1))
        pass_on(f"ogA2{j}", block(0, n - 1, k, j, zb, 1), to_a)
        pass_on(f"oB{j}", block(0, n, k, j, zb, 1), core)
        arrived(f"ogB{j}", block(0, n, k, j, za, 1))
        pass_on(f"ogB2{j}", block(n - 1, 1, k, j, za, 1), to_b)
        pass_on(f"oA{j}", block(0, n, k, j, za, 1), core)

    def end_other(j):
        n = CROSS[j]
        arrived(f"ogA2{j}", block(0, n - 1, k, j, z2, 1))
        pass_on(f"oA2{j}", block(0, n - 1, k, j, z2, 1), core)
        arrived(f"ogB2{j}", block(n - 1, 1, k, j, z2, 1))
        pass_on(f"oB2{j}", block(n - 1, 1, k, j, z2, 1), core)

    def end_hidden(j):
        if CROSS[j] == 2:
            arrived(f"agXh{j}", hidden_rows(j, k, 1))
            pass_on(f"oH{j}", hidden_rows(j, k, 1), core)

    flushes = []

    def flush(src, dst):
        copy = pltpu.make_async_copy(src, dst, flush_sems.at[len(flushes)])
        copy.start()
        flushes.append(copy)

    def flush_act(j, plane):
        if BASE[j] < EARLY:
            return
        rows = pl.ds(place(plane, BASE[j]), CHUNKS[j])
        to_rows = pl.ds(place(plane, BASE[j]) - 2 * EARLY, CHUNKS[j])
        for t, out in enumerate((a0_out, a1_out, a2_out)):
            for kk in range(2):
                flush(act.at[t, kk, rows], out.at[to_rows, pl.ds(kk * HALF, HALF)])

    complete = set()

    def own_complete(j):
        if j in complete:
            return
        complete.add(j)
        arrived(f"cOwn{j}", block(0, 3, kp, j, z))
        arrived(f"cB{j}", block(0, 3, kp, j, za))
        arrived(f"cA{j}", block(0, 3, kp, j, zb))
        arrived(f"cA2{j}", block(0, 2, kp, j, z2))
        arrived(f"cB2{j}", block(2, 1, kp, j, z2))
        flush_act(j, 0)

    def other_complete(j):
        n = CROSS[j]
        arrived(f"oOwn{j}", block(0, n, kp, j, z, 1))
        arrived(f"oB{j}", block(0, n, kp, j, za, 1))
        arrived(f"oA{j}", block(0, n, kp, j, zb, 1))
        arrived(f"oA2{j}", block(0, n - 1, kp, j, z2, 1))
        arrived(f"oB2{j}", block(n - 1, 1, kp, j, z2, 1))
        if n == 2:
            arrived(f"oH{j}", hidden_rows(j, kp, 1))
        flush_act(j, 1)

    gi_to = {PAR: to_xl, M0: same["m"], Q0: same["p"], M1: diag["m"], Q1: diag["p"], T0: same["2"], T1: diag["2"]}

    def input_grad(i):
        group = GI_GROUPS[i]
        first, end = group[0] * BLOCK, (group[-1] + 1) * BLOCK
        for j in range(len(CHUNKS)):
            if BASE[j] < end and BASE[j + 1] > first:
                own_complete(j)
        rows = pl.ds(first, end - first)
        act_rows = pl.ds(place(0, first), end - first)
        total = None
        for t, w in enumerate((gw, uw)):
            for kk in range(2):
                term = lax.dot_general(act[t, kk, act_rows], w[:, kk * HALF:(kk + 1) * HALF], TRANS,
                                       preferred_element_type=F32)
                total = term if total is None else total + term
        gi_send[rows] = total.astype(BF16)
        for b in group:
            if b != OWN:
                send(f"gi{b}", gi_send.at[rows_of(b)], gi_recv.at[b], gi_to[b])

    def flush_tokens():
        for way in "mp2":
            arrived(f"gy_{way}_oth0", tokens(at_own[way], 1))
            arrived(f"gy_{way}_oth1", tokens(at_par[way], 1))
        late = pl.ds(2 * EARLY, 2 * (PLANE - EARLY))
        flush(xg.at[0, late], x_out)
        flush(xg.at[1, late], g_out)

    wg_copies = []

    def wg_slot():
        n = len(wg_copies)
        if n >= 4:
            wg_copies[n - 4].wait()
        return n % 4

    def wg_store(src, dst):
        copy = pltpu.make_async_copy(src, dst, wg_sems.at[len(wg_copies)])
        copy.start()
        wg_copies.append(copy)

    early = pl.ds(0, 2 * EARLY)

    def weight_grad_in(t, m):
        i = wg_slot()
        lhs = xg[0, early, m * 256:(m + 1) * 256]
        for kk in range(2):
            wg[i, :, kk * HALF:(kk + 1) * HALF] = lax.dot_general(
                lhs, act[t, kk, early], OVER_TOKENS, preferred_element_type=F32).astype(BF16)
        wg_store(wg.at[i], (p0_out, p1_out)[t].at[pl.ds(m * 256, 256)])

    def weight_grad_down(kk, m):
        i = wg_slot()
        size = min(256, HALF - m * 256)
        wg[i, :size, :WIDTH] = lax.dot_general(
            act[2, kk, early, m * 256:m * 256 + size], xg[1, early], OVER_TOKENS,
            preferred_element_type=F32).astype(BF16)
        wg_store(wg.at[i, pl.ds(0, size), pl.ds(0, WIDTH)], p2_out.at[pl.ds(kk * HALF + m * 256, size)])

    stages = {
        "G2": gather_par, "G3": gather_far, "G4": gather_depth, "G5": gather_other, "GF": flush_tokens,
        "F": forward, "P": add_core, "R": add_relay, "C": activations, "D1": spread_own, "D2": spread_other,
        "D3": end_own, "D4": relay_other, "D5": end_other, "D6": end_hidden, "H": other_complete,
        "E": input_grad, "W": weight_grad_in, "V": weight_grad_down,
    }
    for name, *index in ORDER:
        stages[name](*index)

    total = gi_send[rows_of(OWN)].astype(F32)
    for b in range(1, 8):
        arrived(f"gi{b}", gi_recv.at[b])
        total = total + gi_recv[b].astype(F32)
    gin_out[...] = total.astype(BF16)
    for copy in started:
        copy.wait_send()
    for copy in flushes + wg_copies[-4:]:
        copy.wait()


def per_device(inputs, grad_out, gate_weight, up_weight, down_weight):
    hbm = pl.BlockSpec(memory_space=pl.ANY)
    n = len(NAMES)
    tokens = 2 * PLANE
    late = tokens - 2 * EARLY
    grad_in, x, g, gate_act, up_act, hidden, gate_early, up_early, down_early = pl.pallas_call(
        kernel,
        out_shape=(
            jax.ShapeDtypeStruct((BLOCK, WIDTH), BF16),
            jax.ShapeDtypeStruct((late, WIDTH), BF16),
            jax.ShapeDtypeStruct((late, WIDTH), BF16),
            jax.ShapeDtypeStruct((late, HID), BF16),
            jax.ShapeDtypeStruct((late, HID), BF16),
            jax.ShapeDtypeStruct((late, HID), BF16),
            jax.ShapeDtypeStruct((WIDTH, HID), BF16),
            jax.ShapeDtypeStruct((WIDTH, HID), BF16),
            jax.ShapeDtypeStruct((HID, WIDTH), BF16),
        ),
        in_specs=[hbm] * 5,
        out_specs=(pl.BlockSpec(memory_space=pltpu.VMEM),) + (hbm,) * 8,
        scratch_shapes=[
            pltpu.VMEM((WIDTH, HID), BF16),
            pltpu.VMEM((WIDTH, HID), BF16),
            pltpu.VMEM((HID, WIDTH), BF16),
            pltpu.VMEM((2, tokens, WIDTH), BF16),
            pltpu.VMEM((3, 2, tokens, HALF), BF16),
            pltpu.VMEM((3, PLANE, HALF), BF16),
            pltpu.VMEM((3, PLANE, HALF), BF16),
            pltpu.VMEM((3, PLANE, HALF), BF16),
            pltpu.VMEM((3, PLANE // 4, HALF), BF16),
            pltpu.VMEM((2, 3, PLANE // 4, HALF), BF16),
            pltpu.VMEM((PLANE, WIDTH), BF16),
            pltpu.VMEM((8, BLOCK, WIDTH), BF16),
            pltpu.VMEM((4, 256, HID), BF16),
            pltpu.SemaphoreType.DMA((n,)),
            pltpu.SemaphoreType.DMA((n,)),
            pltpu.SemaphoreType.DMA((5,)),
            pltpu.SemaphoreType.DMA((N_FLUSH,)),
            pltpu.SemaphoreType.DMA((16,)),
        ],
        compiler_params=pltpu.CompilerParams(
            collective_id=0, has_side_effects=True, vmem_limit_bytes=62 * 2**20),
        name="ffn_exchange",
    )(inputs, grad_out, gate_weight, up_weight, down_weight)

    def weight_grad(a, b, rest):
        late_sum = lax.dot_general(a, b, OVER_TOKENS, preferred_element_type=F32)
        return (late_sum + rest.astype(F32)).astype(BF16)

    return (
        grad_in,
        weight_grad(x, gate_act, gate_early),
        weight_grad(x, up_act, up_early),
        weight_grad(hidden, g, down_early),
    )


def solution(mesh):
    in_specs = (
        P(("depth", "col"), "row"),
        P(("depth", "col"), "row"),
        P("row", "col"),
        P("row", "col"),
        P("col", "row"),
    )
    out_specs = (P(("depth", "col"), "row"), P("row", "col"), P("row", "col"), P("col", "row"))
    return jax.shard_map(
        per_device, mesh=mesh, in_specs=in_specs, out_specs=out_specs, check_vma=False
    )
```

```python
import jax
import jax.numpy as jnp
from jax import lax
from jax.experimental import pallas as pl
from jax.experimental.pallas import tpu as pltpu
from jax.sharding import PartitionSpec as P

MESH = pl.DeviceIdType.MESH
BF16, F32 = jnp.bfloat16, jnp.float32
BLOCK = 96
PLANE = 768
EARLY = 384
WIDTH = 1024
HID = 1792
HALF = 896
TRANS = (((1,), (1,)), ((), ()))
OVER_TOKENS = (((0,), (0,)), ((), ()))
OWN, PAR, M0, Q0, M1, Q1, T0, T1 = range(8)
CHUNKS = (64, 128, 192, 192, 192)
BASE = tuple(sum(CHUNKS[:i]) for i in range(len(CHUNKS) + 1))
PIECEWISE = (len(CHUNKS) - 1,)
CROSS = tuple(3 if j in PIECEWISE else 2 for j in range(len(CHUNKS)))
GI_GROUPS = ((OWN, PAR), (M0, Q0), (M1, Q1), (T0, T1))
ORDER = (
    ("G4",), ("F", 0), ("P", 0), ("R", 0), ("G2",), ("F", 1), ("C", 0), ("G3",), ("P", 1), ("D1", 0),
    ("D2", 0), ("F", 2), ("R", 1), ("P", 2), ("C", 1), ("G5",), ("D3", 0), ("D4", 0), ("R", 2), ("D5", 0),
    ("D6", 0), ("D1", 1), ("D2", 1), ("F", 3), ("P", 3), ("C", 2), ("R", 3), ("D3", 1), ("D4", 1), ("D1", 2),
    ("D2", 2), ("F", 4), ("P", 4), ("D5", 1), ("D6", 1), ("H", 0), ("E", 0), ("C", 3), ("R", 4), ("D3", 2),
    ("D4", 2), ("D1", 3), ("D2", 3), ("D5", 2), ("D6", 2), ("E", 1), ("H", 1), ("C", 4), ("D3", 3), ("D4", 3),
    ("D1", 4), ("D2", 4), ("GF",), ("D5", 3), ("D6", 3), ("E", 2), ("H", 2), ("W", 0, 0),
    ("D3", 4), ("W", 0, 2), ("D4", 4), ("W", 1, 0), ("E", 3), ("W", 1, 2),
    ("D5", 4), ("D6", 4), ("V", 0, 0), ("V", 0, 1), ("V", 0, 2), ("H", 3), ("V", 0, 3),
    ("V", 1, 0), ("V", 1, 1), ("V", 1, 2), ("V", 1, 3), ("H", 4),
)
STEPS = (
    "core", "relA", "relB", "finA", "finB", "agA", "agB", "agA2", "agB2", "agX", "agXh",
    "ogA", "ogB", "ogA2", "ogB2", "cOwn", "cB", "cA", "cA2", "cB2", "oOwn", "oB", "oA", "oA2", "oB2", "oH",
)


def names():
    out = ["g_xl", "g_xo", "g_x2"]
    out += [f"gy_{way}_{what}" for way in "mp2" for what in ("own", "par", "oth0", "oth1")]
    out += [f"gi{b}" for b in range(1, 8)]
    for j in range(len(CHUNKS)):
        out += [f"{n}{j}" for n in STEPS if CROSS[j] == 2 or n not in ("agXh", "oH")]
    return {n: i for i, n in enumerate(out)}


NAMES = names()
N_FLUSH = 2 * len(CHUNKS) * 6 + 2


def multiple(value, of):
    return pl.multiple_of(value, of)


def rows_of(block, count=1):
    return pl.ds(block * BLOCK, count * BLOCK)


def place(plane, row):
    return plane * EARLY + row + (EARLY if row >= EARLY else 0)


def kernel(x_in, g_in, gw_in, uw_in, dw_in,
           gin_out, x_out, g_out, a0_out, a1_out, a2_out, p0_out, p1_out, p2_out,
           gw, uw, dw, xg, act, core_send, core_recv, part, relay, final, gi_send, gi_recv, wg,
           send_sems, recv_sems, load_sems, flush_sems, wg_sems):
    d, r, c = lax.axis_index("depth"), lax.axis_index("row"), lax.axis_index("col")
    z, k = r // 2, r % 2
    kp = 1 - k
    xl, y = c // 4, c % 4
    za = (z + 1 + 2 * k) % 4
    zb = (z + 3 - 2 * k) % 4
    z2 = (z + 2) % 4
    core = (d, r + 1 - 2 * k, c)
    to_a, to_b = (d, za * 2 + k, c), (d, zb * 2 + k, c)
    y_m, y_p, y_2 = (y + 3) % 4, (y + 1) % 4, (y + 2) % 4
    same = {w: (d, r, xl * 4 + v) for w, v in (("m", y_m), ("p", y_p), ("2", y_2))}
    diag = {w: (d, r, (1 - xl) * 4 + v) for w, v in (("m", y_m), ("p", y_p), ("2", y_2))}
    to_xl = (d, r, (1 - xl) * 4 + y)
    to_xo = (1 - d, r, (1 - xl) * 4 + y)
    to_x2 = (1 - d, r, c)
    everyone = [core, to_a, to_b, *same.values(), *diag.values(), to_xl, to_xo, to_x2]
    at_own = {"m": Q0, "p": M0, "2": T0}
    at_par = {"m": Q1, "p": M1, "2": T1}

    started = []

    def send(name, src, dst, device):
        i = NAMES[name]
        copy = pltpu.make_async_remote_copy(
            src_ref=src, dst_ref=dst, send_sem=send_sems.at[i], recv_sem=recv_sems.at[i],
            device_id=device, device_id_type=MESH)
        copy.start()
        started.append(copy)

    def arrived(name, dst):
        i = NAMES[name]
        pltpu.make_async_remote_copy(
            src_ref=dst, dst_ref=dst, send_sem=send_sems.at[i], recv_sem=recv_sems.at[i],
            device_id=core, device_id_type=MESH).wait_recv()

    loads = [
        pltpu.make_async_copy(x_in, xg.at[0, rows_of(OWN)], load_sems.at[0]),
        pltpu.make_async_copy(g_in, xg.at[1, rows_of(OWN)], load_sems.at[1]),
        pltpu.make_async_copy(gw_in, gw, load_sems.at[2]),
        pltpu.make_async_copy(uw_in, uw, load_sems.at[3]),
        pltpu.make_async_copy(dw_in, dw, load_sems.at[4]),
    ]
    for load in loads:
        load.start()

    barrier = pltpu.get_barrier_semaphore()
    for device in everyone:
        pl.semaphore_signal(barrier, inc=1, device_id=device, device_id_type=MESH)
    pl.semaphore_wait(barrier, len(everyone))

    def tokens(block, plane=0):
        return xg.at[:, pl.ds(place(plane, block * BLOCK), BLOCK)]

    loads[0].wait()
    loads[1].wait()
    send("g_xl", tokens(OWN), tokens(PAR), to_xl)
    for way in "mp":
        send(f"gy_{way}_own", tokens(OWN), tokens(at_own[way]), same[way])

    def gather_par():
        arrived("g_xl", tokens(PAR))
        for way in "mp":
            send(f"gy_{way}_par", tokens(PAR), tokens(at_par[way]), same[way])

    def gather_far():
        send("gy_2_own", tokens(OWN), tokens(at_own["2"]), same["2"])
        send("gy_2_par", tokens(PAR), tokens(at_par["2"]), same["2"])

    def gather_depth():
        send("g_x2", tokens(OWN), tokens(OWN, 1), to_x2)
        send("g_xo", tokens(OWN), tokens(PAR, 1), to_xo)

    def gather_other():
        arrived("g_x2", tokens(OWN, 1))
        arrived("g_xo", tokens(PAR, 1))
        for way in "mp2":
            send(f"gy_{way}_oth0", tokens(OWN, 1), tokens(at_own[way], 1), same[way])
            send(f"gy_{way}_oth1", tokens(PAR, 1), tokens(at_par[way], 1), same[way])

    seen = set()
    source = {M0: "gy_p_own", Q0: "gy_m_own", M1: "gy_p_par", Q1: "gy_m_par", T0: "gy_2_own", T1: "gy_2_par"}

    def gathered(block):
        if block in source and block not in seen:
            seen.add(block)
            arrived(source[block], tokens(block))

    cols_own = pl.ds(multiple(k * HALF, 128), HALF)
    cols_par = pl.ds(multiple(kp * HALF, 128), HALF)

    def chunk(j):
        return pl.ds(BASE[j], CHUNKS[j])

    def products(j, cols, out):
        here = pl.ds(place(0, BASE[j]), CHUNKS[j])
        x, g = xg[0, here], xg[1, here]
        out[0, chunk(j)] = jnp.dot(x, gw[:, cols], preferred_element_type=F32).astype(BF16)
        out[1, chunk(j)] = jnp.dot(x, uw[:, cols], preferred_element_type=F32).astype(BF16)
        out[2, chunk(j)] = lax.dot_general(g, dw[cols, :], TRANS, preferred_element_type=F32).astype(BF16)

    def piece(j, zz):
        size = CHUNKS[j] // 4
        return pl.ds(multiple(BASE[j] + zz * size, 16), size)

    def act_piece(j, zz, plane=0):
        size = CHUNKS[j] // 4
        return pl.ds(multiple(place(plane, BASE[j]) + zz * size, 16), size)

    def slot(j):
        return pl.ds(BASE[j] // 4, CHUNKS[j] // 4)

    def whole(j):
        return core_recv.at[:, chunk(j)]

    def forward(j):
        for b in range(8):
            if b * BLOCK < BASE[j + 1] and (b + 1) * BLOCK > BASE[j]:
                gathered(b)
        if j == 0:
            for load in loads[2:]:
                load.wait()
        products(j, cols_par, core_send)
        send(f"core{j}", core_send.at[:, chunk(j)], whole(j), core)
        products(j, cols_own, part)

    def add_core(j):
        arrived(f"core{j}", whole(j))

        def add(zz):
            rows = piece(j, zz)
            part[:, rows] = (part[:, rows].astype(F32) + core_recv[:, rows].astype(F32)).astype(BF16)

        add(z2)
        send(f"relA{j}", part.at[pl.ds(0, 2), piece(j, z2)], relay.at[pl.ds(0, 2), slot(j)], to_a)
        send(f"relB{j}", part.at[pl.ds(2, 1), piece(j, z2)], relay.at[pl.ds(2, 1), slot(j)], to_b)
        add(za)
        add(zb)
        add(z)

    def add_relay(j):
        rows_a, rows_b = piece(j, za), piece(j, zb)
        arrived(f"relA{j}", relay.at[pl.ds(0, 2), slot(j)])
        part[0:2, rows_a] = (part[0:2, rows_a].astype(F32) + relay[0:2, slot(j)].astype(F32)).astype(BF16)
        send(f"finA{j}", part.at[:, rows_a], final.at[0, :, slot(j)], to_a)
        arrived(f"relB{j}", relay.at[pl.ds(2, 1), slot(j)])
        part[2:3, rows_b] = (part[2:3, rows_b].astype(F32) + relay[2:3, slot(j)].astype(F32)).astype(BF16)
        send(f"finB{j}", part.at[:, rows_b], final.at[1, :, slot(j)], to_b)

    def block(t, n, kk, j, zz, plane=0):
        return act.at[pl.ds(t, n), kk, act_piece(j, zz, plane)]

    def pass_on(name, ref, device):
        send(name, ref, ref, device)

    def activations(j):
        arrived(f"finA{j}", final.at[0, :, slot(j)])
        arrived(f"finB{j}", final.at[1, :, slot(j)])
        mine = piece(j, z)
        gate, up, grad = (
            part[t, mine].astype(F32) + final[0, t, slot(j)].astype(F32) + final[1, t, slot(j)].astype(F32)
            for t in range(3))
        sig = jax.nn.sigmoid(gate)
        here = act_piece(j, z)
        act[0, k, here] = (grad * up * sig * (1.0 + gate * (1.0 - sig))).astype(BF16)
        act[1, k, here] = (grad * gate * sig).astype(BF16)
        act[2, k, here] = (gate * sig * up).astype(BF16)
        pass_on(f"agA{j}", block(0, 3, k, j, z), to_a)
        pass_on(f"agB{j}", block(0, 3, k, j, z), to_b)
        send(f"agX{j}", block(0, CROSS[j], k, j, z), block(0, CROSS[j], k, j, z, 1), to_x2)
        pass_on(f"cOwn{j}", block(0, 3, k, j, z), core)

    def spread_own(j):
        arrived(f"agA{j}", block(0, 3, k, j, zb))
        pass_on(f"agA2{j}", block(0, 2, k, j, zb), to_a)
        pass_on(f"cB{j}", block(0, 3, k, j, zb), core)
        arrived(f"agB{j}", block(0, 3, k, j, za))
        pass_on(f"agB2{j}", block(2, 1, k, j, za), to_b)
        pass_on(f"cA{j}", block(0, 3, k, j, za), core)

    def spread_other(j):
        mine = block(0, CROSS[j], k, j, z, 1)
        arrived(f"agX{j}", mine)
        pass_on(f"ogA{j}", mine, to_a)
        pass_on(f"ogB{j}", mine, to_b)
        pass_on(f"oOwn{j}", mine, core)

    def hidden_rows(j, kk, plane):
        return act.at[2, kk, pl.ds(place(plane, BASE[j]), CHUNKS[j])]

    def end_own(j):
        arrived(f"agA2{j}", block(0, 2, k, j, z2))
        pass_on(f"cA2{j}", block(0, 2, k, j, z2), core)
        arrived(f"agB2{j}", block(2, 1, k, j, z2))
        pass_on(f"cB2{j}", block(2, 1, k, j, z2), core)
        if CROSS[j] == 2:
            send(f"agXh{j}", hidden_rows(j, k, 0), hidden_rows(j, k, 1), to_x2)

    def relay_other(j):
        n = CROSS[j]
        arrived(f"ogA{j}", block(0, n, k, j, zb, 1))
        pass_on(f"ogA2{j}", block(0, n - 1, k, j, zb, 1), to_a)
        pass_on(f"oB{j}", block(0, n, k, j, zb, 1), core)
        arrived(f"ogB{j}", block(0, n, k, j, za, 1))
        pass_on(f"ogB2{j}", block(n - 1, 1, k, j, za, 1), to_b)
        pass_on(f"oA{j}", block(0, n, k, j, za, 1), core)

    def end_other(j):
        n = CROSS[j]
        arrived(f"ogA2{j}", block(0, n - 1, k, j, z2, 1))
        pass_on(f"oA2{j}", block(0, n - 1, k, j, z2, 1), core)
        arrived(f"ogB2{j}", block(n - 1, 1, k, j, z2, 1))
        pass_on(f"oB2{j}", block(n - 1, 1, k, j, z2, 1), core)

    def end_hidden(j):
        if CROSS[j] == 2:
            arrived(f"agXh{j}", hidden_rows(j, k, 1))
            pass_on(f"oH{j}", hidden_rows(j, k, 1), core)

    flushes = []

    def flush(src, dst):
        copy = pltpu.make_async_copy(src, dst, flush_sems.at[len(flushes)])
        copy.start()
        flushes.append(copy)

    def flush_act(j, plane):
        if BASE[j] < EARLY:
            return
        rows = pl.ds(place(plane, BASE[j]), CHUNKS[j])
        to_rows = pl.ds(place(plane, BASE[j]) - 2 * EARLY, CHUNKS[j])
        for t, out in enumerate((a0_out, a1_out, a2_out)):
            for kk in range(2):
                flush(act.at[t, kk, rows], out.at[to_rows, pl.ds(kk * HALF, HALF)])

    complete = set()

    def own_complete(j):
        if j in complete:
            return
        complete.add(j)
        arrived(f"cOwn{j}", block(0, 3, kp, j, z))
        arrived(f"cB{j}", block(0, 3, kp, j, za))
        arrived(f"cA{j}", block(0, 3, kp, j, zb))
        arrived(f"cA2{j}", block(0, 2, kp, j, z2))
        arrived(f"cB2{j}", block(2, 1, kp, j, z2))
        flush_act(j, 0)

    def other_complete(j):
        n = CROSS[j]
        arrived(f"oOwn{j}", block(0, n, kp, j, z, 1))
        arrived(f"oB{j}", block(0, n, kp, j, za, 1))
        arrived(f"oA{j}", block(0, n, kp, j, zb, 1))
        arrived(f"oA2{j}", block(0, n - 1, kp, j, z2, 1))
        arrived(f"oB2{j}", block(n - 1, 1, kp, j, z2, 1))
        if n == 2:
            arrived(f"oH{j}", hidden_rows(j, kp, 1))
        flush_act(j, 1)

    gi_to = {PAR: to_xl, M0: same["m"], Q0: same["p"], M1: diag["m"], Q1: diag["p"], T0: same["2"], T1: diag["2"]}

    def input_grad(i):
        group = GI_GROUPS[i]
        first, end = group[0] * BLOCK, (group[-1] + 1) * BLOCK
        for j in range(len(CHUNKS)):
            if BASE[j] < end and BASE[j + 1] > first:
                own_complete(j)
        rows = pl.ds(first, end - first)
        act_rows = pl.ds(place(0, first), end - first)
        total = None
        for t, w in enumerate((gw, uw)):
            for kk in range(2):
                term = lax.dot_general(act[t, kk, act_rows], w[:, kk * HALF:(kk + 1) * HALF], TRANS,
                                       preferred_element_type=F32)
                total = term if total is None else total + term
        gi_send[rows] = total.astype(BF16)
        for b in group:
            if b != OWN:
                send(f"gi{b}", gi_send.at[rows_of(b)], gi_recv.at[b], gi_to[b])

    def flush_tokens():
        for way in "mp2":
            arrived(f"gy_{way}_oth0", tokens(at_own[way], 1))
            arrived(f"gy_{way}_oth1", tokens(at_par[way], 1))
        late = pl.ds(2 * EARLY, 2 * (PLANE - EARLY))
        flush(xg.at[0, late], x_out)
        flush(xg.at[1, late], g_out)

    wg_copies = []

    def wg_slot():
        n = len(wg_copies)
        if n >= 4:
            wg_copies[n - 4].wait()
        return n % 4

    def wg_store(src, dst):
        copy = pltpu.make_async_copy(src, dst, wg_sems.at[len(wg_copies)])
        copy.start()
        wg_copies.append(copy)

    early = pl.ds(0, 2 * EARLY)

    def weight_grad_in(t, m):
        n = len(wg_copies)
        for copy in wg_copies[max(n - 4, 0):max(n - 2, 0)]:
            copy.wait()

        def tile(i, carry):
            lhs = xg[0, early, pl.ds(multiple((m + i) * 256, 256), 256)]
            for kk in range(2):
                wg[n % 4 + i, :, kk * HALF:(kk + 1) * HALF] = lax.dot_general(
                    lhs, act[t, kk, early], OVER_TOKENS, preferred_element_type=F32).astype(BF16)
            return carry

        lax.fori_loop(0, 2, tile, 0)
        for i in range(2):
            wg_store(wg.at[n % 4 + i], (p0_out, p1_out)[t].at[pl.ds((m + i) * 256, 256)])

    def weight_grad_down(kk, m):
        i = wg_slot()
        size = min(256, HALF - m * 256)
        wg[i, :size, :WIDTH] = lax.dot_general(
            act[2, kk, early, m * 256:m * 256 + size], xg[1, early], OVER_TOKENS,
            preferred_element_type=F32).astype(BF16)
        wg_store(wg.at[i, pl.ds(0, size), pl.ds(0, WIDTH)], p2_out.at[pl.ds(kk * HALF + m * 256, size)])

    stages = {
        "G2": gather_par, "G3": gather_far, "G4": gather_depth, "G5": gather_other, "GF": flush_tokens,
        "F": forward, "P": add_core, "R": add_relay, "C": activations, "D1": spread_own, "D2": spread_other,
        "D3": end_own, "D4": relay_other, "D5": end_other, "D6": end_hidden, "H": other_complete,
        "E": input_grad, "W": weight_grad_in, "V": weight_grad_down,
    }
    for name, *index in ORDER:
        stages[name](*index)

    total = gi_send[rows_of(OWN)].astype(F32)
    for b in range(1, 8):
        arrived(f"gi{b}", gi_recv.at[b])
        total = total + gi_recv[b].astype(F32)
    gin_out[...] = total.astype(BF16)
    for copy in started:
        copy.wait_send()
    for copy in flushes + wg_copies[-4:]:
        copy.wait()


def per_device(inputs, grad_out, gate_weight, up_weight, down_weight):
    hbm = pl.BlockSpec(memory_space=pl.ANY)
    n = len(NAMES)
    tokens = 2 * PLANE
    late = tokens - 2 * EARLY
    grad_in, x, g, gate_act, up_act, hidden, gate_early, up_early, down_early = pl.pallas_call(
        kernel,
        out_shape=(
            jax.ShapeDtypeStruct((BLOCK, WIDTH), BF16),
            jax.ShapeDtypeStruct((late, WIDTH), BF16),
            jax.ShapeDtypeStruct((late, WIDTH), BF16),
            jax.ShapeDtypeStruct((late, HID), BF16),
            jax.ShapeDtypeStruct((late, HID), BF16),
            jax.ShapeDtypeStruct((late, HID), BF16),
            jax.ShapeDtypeStruct((WIDTH, HID), BF16),
            jax.ShapeDtypeStruct((WIDTH, HID), BF16),
            jax.ShapeDtypeStruct((HID, WIDTH), BF16),
        ),
        in_specs=[hbm] * 5,
        out_specs=(pl.BlockSpec(memory_space=pltpu.VMEM),) + (hbm,) * 8,
        scratch_shapes=[
            pltpu.VMEM((WIDTH, HID), BF16),
            pltpu.VMEM((WIDTH, HID), BF16),
            pltpu.VMEM((HID, WIDTH), BF16),
            pltpu.VMEM((2, tokens, WIDTH), BF16),
            pltpu.VMEM((3, 2, tokens, HALF), BF16),
            pltpu.VMEM((3, PLANE, HALF), BF16),
            pltpu.VMEM((3, PLANE, HALF), BF16),
            pltpu.VMEM((3, PLANE, HALF), BF16),
            pltpu.VMEM((3, PLANE // 4, HALF), BF16),
            pltpu.VMEM((2, 3, PLANE // 4, HALF), BF16),
            pltpu.VMEM((PLANE, WIDTH), BF16),
            pltpu.VMEM((8, BLOCK, WIDTH), BF16),
            pltpu.VMEM((4, 256, HID), BF16),
            pltpu.SemaphoreType.DMA((n,)),
            pltpu.SemaphoreType.DMA((n,)),
            pltpu.SemaphoreType.DMA((5,)),
            pltpu.SemaphoreType.DMA((N_FLUSH,)),
            pltpu.SemaphoreType.DMA((16,)),
        ],
        compiler_params=pltpu.CompilerParams(
            collective_id=0, has_side_effects=True, vmem_limit_bytes=62 * 2**20),
        name="ffn_exchange",
    )(inputs, grad_out, gate_weight, up_weight, down_weight)

    def weight_grad(a, b, rest):
        late_sum = lax.dot_general(a, b, OVER_TOKENS, preferred_element_type=F32)
        return (late_sum + rest.astype(F32)).astype(BF16)

    return (
        grad_in,
        weight_grad(x, gate_act, gate_early),
        weight_grad(x, up_act, up_early),
        weight_grad(hidden, g, down_early),
    )


def solution(mesh):
    in_specs = (
        P(("depth", "col"), "row"),
        P(("depth", "col"), "row"),
        P("row", "col"),
        P("row", "col"),
        P("col", "row"),
    )
    out_specs = (P(("depth", "col"), "row"), P("row", "col"), P("row", "col"), P("col", "row"))
    return jax.shard_map(
        per_device, mesh=mesh, in_specs=in_specs, out_specs=out_specs, check_vma=False
    )
```
